32 devices in a mesh: seq: 8 (over z, x), heads: 2 (over core), dp: 2 (over y).
Axes of the slice: x: 2, y: 2, z: 4, core: 2. Of those that a mesh axis runs over, the one named last changes fastest.
Arguments:
- queries: bfloat16 [2048, 2048], P(('dp', 'seq'), 'heads'), parts along dimension 0, may hold values from -6 to 6
- keys: bfloat16 [2048, 512], P(('dp', 'seq'), 'heads'), parts along dimension 0, may hold values from -6 to 6
- values: bfloat16 [2048, 512], P(('dp', 'seq'), 'heads'), parts along dimension 0, may hold values from -6 to 6
- house: bfloat16 [2048, 512], P(('dp', 'seq'), 'heads'), parts along dimension 0, may hold values from -16 to 16
- beta: float32 [4, 2048], P('heads', ('dp', 'seq')), parts along dimension 1, may hold values from 0.5 to 1.5
- out_weight: bfloat16 [2048, 2048], P('heads'), may hold values from -2 to 2
Outputs:
- mixed: bfloat16 [2048, 2048], P(('dp', 'seq'), 'heads'), parts along dimension 0
The draws below stay inside these ranges and needn't reach their ends.
There are 2 independent parts, one for each index of `dp`. The reference program is written for one: setup_inputs(seed, part) draws one part's arguments, and reference() takes and returns one part's arrays. A program takes and returns all parts, laid end to end along the dimension named above; an argument that names none is the same for every part. Nothing has to cross between parts.
All inputs are finite; a program needn't handle non-finite values.
Results may differ from the reference program's by a relative error of at most 0.012.
Values may be sent and summed in bfloat16 or wider, within the bound.
A program may use at most 64 MiB of HBM per device.

```python
import math
import jax
import jax.numpy as jnp
from jax import lax

HD = 128
QH = 16
KVH = 4
DW = 2048
TOK_DEV = 128
SEQLEN = 1024


def draw_queries(key, part):
    normal = jax.random.normal(jax.random.fold_in(key, 1), (SEQLEN, QH * HD), jnp.float32)
    rows_out = jnp.clip(normal * 1.5, -6.0, 6.0)
    return rows_out.astype(jnp.bfloat16)


def draw_keys(key, part):
    normal = jax.random.normal(jax.random.fold_in(key, 21), (SEQLEN, KVH * HD), jnp.float32)
    rows_out = jnp.clip(normal, -6.0, 6.0)
    return rows_out.astype(jnp.bfloat16)


def draw_house(key, part):
    blocks = SEQLEN // TOK_DEV
    slow_share = 0.6
    slow_count = max(1, min(HD - 1, int(slow_share * HD)))
    order_keys = jax.random.split(jax.random.fold_in(key, 4), KVH)
    ranks = jax.vmap(lambda one_key: jax.random.permutation(one_key, HD))(order_keys)
    is_slow = ranks < slow_count
    slow_rate = jnp.exp(jax.random.uniform(jax.random.fold_in(key, 8), (KVH, HD), jnp.float32, math.log(1.0 / blocks), math.log(2.0 / blocks)))
    fast_raw = jnp.exp(jax.random.uniform(jax.random.fold_in(key, 9), (KVH, HD), jnp.float32, 0.0, math.log(8.0)))
    slow_sum = jnp.sum(jnp.where(is_slow, slow_rate, 0.0), axis=1, keepdims=True)
    fast_sum = jnp.sum(jnp.where(is_slow, 0.0, fast_raw), axis=1, keepdims=True)
    fast_budget = jnp.maximum(TOK_DEV - slow_sum, 0.5 * TOK_DEV)
    fast_rate = fast_raw * fast_budget / fast_sum
    target = jnp.where(is_slow, slow_rate, fast_rate)
    base_scale = jnp.sqrt(target / jnp.max(target, axis=1, keepdims=True))
    factors = jnp.exp(jax.random.uniform(jax.random.fold_in(key, 5), (blocks, KVH, HD), jnp.float32, -0.35, 0.35))
    noise = jnp.clip(jax.random.normal(jax.random.fold_in(key, 6), (SEQLEN, KVH, HD), jnp.float32), -6.0, 6.0)
    steady = noise * jnp.repeat(factors, TOK_DEV, axis=0) * base_scale[None]
    starts = jax.random.randint(jax.random.fold_in(key, 7), (4,), 0, SEQLEN - 24)
    places = jnp.arange(SEQLEN)
    bursting = jnp.any((places[:, None] >= starts[None, :]) & (places[:, None] < starts[None, :] + 24), axis=1)
    slow_rows = noise * (jnp.min(base_scale, axis=1, keepdims=True) / base_scale)[None]
    rows_out = jnp.where(bursting[:, None, None], slow_rows, steady)
    return rows_out.reshape(SEQLEN, KVH * HD).astype(jnp.bfloat16)


def spiked(values, stream_key, source, target, blocks, factor):
    owner, partner = [(jnp.arange(values.shape[dim]) // (values.shape[dim] // blocks)).reshape([-1 if axis == dim else 1 for axis in range(values.ndim)]) for dim in (source, target)]
    chosen = jax.random.permutation(stream_key, blocks)[partner]
    strong = (owner == chosen) | (owner == (partner + blocks // 2) % blocks)
    return jnp.where(strong, factor * values, values)


def block_levels(rng, dims, pieces, low, top_value):
    loudness = 1.0
    for dim, parts in pieces:
        draws = jax.random.uniform(jax.random.fold_in(jax.random.fold_in(rng, 6), dim), (parts,), jnp.float32, low / len(pieces), top_value / len(pieces))
        loudness = loudness * jnp.repeat(jnp.exp(draws), dims[dim] // parts).reshape((-1,) + (1,) * (len(dims) - 1 - dim))
    return loudness


def gaussian(rng, extent, scale, bound, cuts=(), kind=jnp.bfloat16):
    values = jax.random.normal(rng, extent, jnp.float32) * scale
    if len(cuts) > 0:
        values = block_levels(rng, extent, cuts, -0.22, 0.18) * values
    return jnp.clip(values, min=-bound, max=bound).astype(kind)


def heavy_noise(key, dims, width, most, cuts, heavy, kind=jnp.bfloat16):
    values = width * jax.random.normal(key, dims, jnp.float32)
    if cuts:
        values = values * block_levels(key, dims, cuts, -0.22, 0.18)
    return jnp.clip(spiked(values, jax.random.fold_in(key, 3), *heavy), -most, most).astype(kind)


def setup_inputs(seed: int = 0, part: int = 0) -> dict:
    splits = jax.random.split(jax.random.key(seed), 7)
    own_keys = jax.random.split(jax.random.fold_in(splits[6], part), 7)
    return {
        "queries": draw_queries(jax.random.fold_in(jax.random.fold_in(splits[6], part), 71), part),
        "keys": draw_keys(jax.random.fold_in(jax.random.fold_in(splits[6], part), 71), part),
        "values": gaussian(own_keys[2], (SEQLEN, KVH * HD), 1.0, 6.0, ((0, 8), (1, 2))),
        "house": draw_house(jax.random.fold_in(jax.random.fold_in(splits[6], part), 71), part),
        "beta": jnp.clip(0.5 + 1.0 * jax.random.uniform(own_keys[4], (KVH, SEQLEN), jnp.float32) ** block_levels(own_keys[4], (KVH, SEQLEN), ((0, 2), (1, 8)), -0.2, 0.2), 0.5, 1.5),
        "out_weight": heavy_noise(splits[5], (QH * HD, DW), (HD // 8) ** -0.5, 2.0, ((0, 2),), (0, 1, 2, 2.0)),
    }


highest = lax.Precision.HIGHEST
norm_floor = 1e-06
masked_score = -1e+30

def rounded(values_in):
    return lax.optimization_barrier(values_in.astype(jnp.bfloat16)).astype(jnp.float32)

def unit_vectors(house_rows):
    return house_rows / jnp.sqrt(lax.optimization_barrier(jnp.sum(house_rows * house_rows, axis=-1, keepdims=True)) + norm_floor)

def block_local(query_rows, key_rows, vectors, betas):
    rows_dev, groups, per_group, head_size = query_rows.shape
    start_keys = jnp.zeros((groups, rows_dev, head_size), jnp.float32)
    start_product = jnp.broadcast_to(jnp.eye(head_size, dtype=jnp.float32), (groups, head_size, head_size))

    def token_step(loop_carry, inputs):
        moved_keys, product = loop_carry
        query_row, key_row, vector, beta_row, position = inputs
        along_vector = jnp.einsum('gjd,gd->gj', moved_keys, vector, precision=highest)
        moved_keys = moved_keys - beta_row[:, None, None] * along_vector[:, :, None] * vector[:, None, :]
        moved_keys = lax.dynamic_update_slice(moved_keys, key_row[:, None, :], (jnp.int32(0), position, jnp.int32(0)))
        across = jnp.einsum('gd,gde->ge', vector, product, precision=highest)
        product = product - beta_row[:, None, None] * vector[:, :, None] * across[:, None, :]
        scores = jnp.einsum('gqd,gjd->gqj', query_row, moved_keys, precision=highest)
        turned = jnp.einsum('gab,gqa->gqb', product, query_row, precision=highest)
        return ((moved_keys, product), (scores, turned))
    positions = jnp.arange(rows_dev, dtype=jnp.int32)
    (moved_keys, product), (scores, turned) = lax.scan(token_step, (start_keys, start_product), (query_rows, key_rows, vectors, betas, positions))
    return (scores, turned, moved_keys, product)

def reference(queries, keys, values, house, beta, out_weight):
    groups = KVH
    per_group = QH // KVH
    blocks = SEQLEN // TOK_DEV
    score_scale = 1.0 / math.sqrt(HD)
    query_all = queries.astype(jnp.float32).reshape(blocks, TOK_DEV, groups, per_group, HD)
    key_all = keys.astype(jnp.float32).reshape(blocks, TOK_DEV, groups, HD)
    vector_all = unit_vectors(house.astype(jnp.float32).reshape(blocks, TOK_DEV, groups, HD))
    beta_all = jnp.transpose(beta).reshape(blocks, TOK_DEV, groups)
    value_all = values.astype(jnp.float32).reshape(SEQLEN, groups, HD)
    offsets = jnp.arange(TOK_DEV, dtype=jnp.int32)
    causal = offsets[None, :] <= offsets[:, None]
    columns = jnp.arange(SEQLEN, dtype=jnp.int32)

    def per_block(carried, inputs):
        query_rows, key_rows, vector_rows, beta_rows, block_index = inputs
        scores, turned, moved_keys, product = block_local(query_rows, key_rows, vector_rows, beta_rows)
        start = (block_index * TOK_DEV).astype(jnp.int32)
        local_scores = jnp.where(causal[:, None, None, :], scores * score_scale, masked_score)
        far_scores = jnp.einsum('tgqd,jgd->tgqj', rounded(turned), rounded(carried), precision=highest) * score_scale
        far_scores = jnp.where((columns < start)[None, None, None, :], far_scores, masked_score)
        row_max = jnp.maximum(lax.optimization_barrier(jnp.max(local_scores, axis=-1, keepdims=True)), lax.optimization_barrier(jnp.max(far_scores, axis=-1, keepdims=True)))
        near_weights = jnp.exp(local_scores - row_max)
        far_weights = jnp.exp(far_scores - row_max)
        row_total = lax.optimization_barrier(jnp.sum(near_weights, axis=-1, keepdims=True)) + lax.optimization_barrier(jnp.sum(far_weights, axis=-1, keepdims=True))
        near_values = lax.dynamic_slice_in_dim(value_all, start, TOK_DEV, 0)
        weighted = jnp.einsum('tgqj,jgd->tgqd', rounded(near_weights), near_values, precision=highest)
        weighted = weighted + jnp.einsum('tgqj,jgd->tgqd', rounded(far_weights), value_all, precision=highest)
        attended = (weighted / row_total).astype(jnp.bfloat16).reshape(TOK_DEV, QH * HD)
        block_map = rounded(product)
        carried = jnp.einsum('gba,jga->jgb', block_map, carried, precision=highest)
        block_ends = rounded(jnp.transpose(moved_keys, (1, 0, 2)))
        carried = lax.dynamic_update_slice(carried, block_ends, (start, jnp.int32(0), jnp.int32(0)))
        return (carried, attended)
    start_carry = jnp.zeros((SEQLEN, groups, HD), jnp.float32)
    block_ids = jnp.arange(blocks, dtype=jnp.int32)
    ending, attended = lax.scan(per_block, start_carry, (query_all, key_all, vector_all, beta_all, block_ids))
    attended = attended.reshape(SEQLEN, QH * HD)
    return jnp.dot(attended, out_weight, preferred_element_type=jnp.float32).astype(jnp.bfloat16)
```

```python
import functools
import math

import jax
import jax.numpy as jnp
from jax import lax
from jax.experimental import pallas as pl
from jax.experimental.pallas import tpu as pltpu
from jax.sharding import PartitionSpec as P

HD = 128
norm_floor = 1e-06
masked_score = -1e30
MESH = pl.DeviceIdType.MESH
f32 = jnp.float32
bf16 = jnp.bfloat16


def split(a):
    hi = a.astype(bf16)
    return hi, (a - hi.astype(f32)).astype(bf16)


def dot(a, b):
    return jnp.dot(a, b, preferred_element_type=f32)


def dot_two(ah, al, b):
    return dot(jnp.concatenate([ah, al], 1), jnp.concatenate([b, b], 0))


def dot_three(ah, al, bh, bl):
    return dot_two(ah, al, bh) + dot(ah, bl)


def kernel(n, cols, peers, groups, per_group, chunks, *refs):
    (q_ref, k_ref, v_ref, h_ref, beta_ref, w_hbm, o_ref,
     w_ref, own, far, vals, turned_ref, prod_ref, max_ref, sum_ref, acc_ref,
     part_out, part_in,
     w_sem, v_send, v_send_row, v_rel, v_recv, e_send, e_send_row, e_rel, e_recv,
     p_send, p_recv) = refs
    rows = n // cols
    tok = q_ref.shape[0]
    me = lax.axis_index("seq")
    head = lax.axis_index("heads")
    z = lax.div(me, cols)
    x = lax.rem(me, cols)

    def copy_w(j):
        width = w_ref.shape[1] // peers
        at = pl.ds(j * width, width)
        return pltpu.make_async_copy(w_hbm.at[:, at], w_ref.at[:, at], w_sem.at[j])

    for j in range(peers):
        copy_w(j).start()

    barrier = pltpu.get_barrier_semaphore()
    for dz in range(1, rows):
        there = lax.rem(z + dz, rows) * cols + x
        pl.semaphore_signal(barrier, inc=1, device_id={"seq": there}, device_id_type=MESH)
    for dx in range(1, cols):
        there = z * cols + lax.rem(x + dx, cols)
        pl.semaphore_signal(barrier, inc=1, device_id={"seq": there}, device_id_type=MESH)
    for dh in range(1, peers):
        there = lax.rem(head + dh, peers)
        pl.semaphore_signal(barrier, inc=1, device_id={"heads": there}, device_id_type=MESH)
    pl.semaphore_wait(barrier, rows + cols + peers - 3)

    def column_copy(source, slots, send, recv, z2):
        return pltpu.make_async_remote_copy(
            src_ref=source, dst_ref=slots.at[me], send_sem=send.at[z2], recv_sem=recv.at[me],
            device_id={"seq": z2 * cols + x}, device_id_type=MESH)

    def row_copy(source, slots, send, recv, x2):
        return pltpu.make_async_remote_copy(
            src_ref=source, dst_ref=slots.at[me], send_sem=send.at[x2], recv_sem=recv.at[me],
            device_id={"seq": z * cols + x2}, device_id_type=MESH)

    def relay_copy(slots, send, recv, zr, dx):
        block = zr * cols + x
        return pltpu.make_async_remote_copy(
            src_ref=slots.at[block], dst_ref=slots.at[block], send_sem=send.at[zr, dx],
            recv_sem=recv.at[block],
            device_id={"seq": z * cols + lax.rem(x + dx, cols)}, device_id_type=MESH)

    def wait_block(slots, recv, block):
        pltpu.make_async_remote_copy(
            src_ref=slots.at[block], dst_ref=slots.at[block], send_sem=w_sem.at[0],
            recv_sem=recv.at[block], device_id={"heads": lax.rem(head + 1, peers)},
            device_id_type=MESH).wait_recv()

    def loop(lower, upper, body):
        def step(i, carry):
            body(i)
            return carry
        lax.fori_loop(lower, upper, step, 0)

    def send_all(source, slots, send, send_row, recv):
        loop(x + 1, cols, lambda x2: row_copy(source, slots, send_row, recv, x2).start())
        loop(z + 1, rows, lambda z2: column_copy(source, slots, send, recv, z2).start())

    def sent_all(source, slots, send, send_row, rel, recv):
        loop(x + 1, cols, lambda x2: row_copy(source, slots, send_row, recv, x2).wait_send())
        loop(z + 1, rows, lambda z2: column_copy(source, slots, send, recv, z2).wait_send())

        def one(zr):
            for dx in range(1, cols):
                relay_copy(slots, rel, recv, zr, dx).wait_send()
        loop(0, z, one)

    def relay(slots, rel, recv, zr):
        wait_block(slots, recv, zr * cols + x)
        for dx in range(1, cols):
            relay_copy(slots, rel, recv, zr, dx).start()

    send_all(v_ref, vals, v_send, v_send_row, v_recv)

    row = lax.broadcasted_iota(jnp.int32, (tok, tok), 0)
    col = lax.broadcasted_iota(jnp.int32, (tok, tok), 1)
    diag = row == col
    eye = diag.astype(f32)
    below = col < row
    differ = row ^ col
    upto = jnp.concatenate([col <= row] * per_group, 0)
    scale = math.log2(math.e) / math.sqrt(HD)
    span = range(groups)

    def lanes(g):
        return slice(g * HD, (g + 1) * HD)

    h = [h_ref[:, lanes(g)] for g in span]
    k = [k_ref[:, lanes(g)] for g in span]
    q = [jnp.concatenate([q_ref[:, lanes(g * per_group + i)] for i in range(per_group)], 0)
         for g in span]
    h_t = [h[g].T for g in span]
    k_t = [k[g].T for g in span]
    hk_t = [jnp.concatenate([h_t[g], k_t[g]], 1) for g in span]
    first = [dot(h[g], hk_t[g]) for g in span]
    gram = [first[g][:, :tok] for g in span]
    square = [jnp.where(diag, gram[g], 0.0) for g in span]
    s_col = [lax.rsqrt(jnp.sum(square[g], 1, keepdims=True) + norm_floor) for g in span]
    s_row = [lax.rsqrt(jnp.sum(square[g], 0, keepdims=True) + norm_floor) for g in span]
    beta_row = [beta_ref[g:g + 1, :] for g in span]
    beta_col = [jnp.sum(jnp.where(diag, beta_row[g], 0.0), 1, keepdims=True) for g in span]
    strict = [jnp.where(below, gram[g] * (s_col[g] * beta_col[g]) * s_row[g], 0.0) for g in span]
    key_along = [jnp.where(below, first[g][:, tok:] * s_col[g], 0.0) for g in span]
    parts = [split(strict[g]) for g in span]
    inverse = [eye - jnp.where(differ == 1, strict[g], 0.0) for g in span]
    size = 2
    while size < tok:
        mask = (differ >= size) & (differ < 2 * size)
        halves = [split(inverse[g]) for g in span]
        zero = jnp.zeros((tok, tok), bf16)
        inner = [dot_three(jnp.where(mask, parts[g][0], zero), jnp.where(mask, parts[g][1], zero),
                           *halves[g]) for g in span]
        inner = [split(inner[g]) for g in span]
        inverse = [inverse[g] - dot_three(*halves[g], *inner[g]) for g in span]
        size *= 2
    solver = [split(inverse[g] * beta_row[g]) for g in span]
    right = [split(jnp.concatenate([h[g].astype(f32) * s_col[g], key_along[g]], 1)) for g in span]
    solved = [dot_three(*solver[g], *right[g]) for g in span]
    scaled = [split(solved[g] * s_col[g]) for g in span]
    for g in span:
        base = jnp.concatenate([eye, k_t[g].astype(f32)], 1)
        turn = dot(jnp.concatenate([h_t[g], h_t[g]], 1), jnp.concatenate(scaled[g], 0))
        own[g * HD:(g + 1) * HD, :] = (base - turn).astype(bf16)
    send_all(own, far, e_send, e_send_row, e_recv)

    for g in span:
        second = dot(q[g], hk_t[g])
        along = split(jnp.where(upto, second[:, :tok] * s_row[g], 0.0))
        base = jnp.concatenate([q[g].astype(f32), second[:, tok:]], 1)
        both = base - dot_three(*along, *split(solved[g]))
        turned_ref[g] = both[:, :HD].astype(bf16)
        score = jnp.where(upto, both[:, HD:] * scale, masked_score)
        top = jnp.max(score, 1, keepdims=True)
        expo = jnp.exp2(score - top)
        max_ref[g] = jnp.broadcast_to(top, max_ref.shape[1:])
        sum_ref[g] = expo
        acc_ref[g] = dot(expo.astype(bf16), v_ref[:, lanes(g)])
        prod_ref[g] = eye

    loop(0, z, lambda i: relay(vals, v_rel, v_recv, z - 1 - i))

    def absorb(i):
        block = me - 1 - i
        zr = lax.div(block, cols)
        xr = lax.rem(block, cols)
        earlier = zr < z

        @pl.when(earlier & (xr == cols - 1))
        def _():
            relay(far, e_rel, e_recv, zr)

        @pl.when(jnp.logical_not(earlier & (xr == x)))
        def _():
            wait_block(vals, v_recv, block)
            wait_block(far, e_recv, block)

        for g in span:
            moved = dot_two(*split(prod_ref[g]), far[block, g * HD:(g + 1) * HD, :])
            prod_ref[g] = moved[:, :HD]
            score = dot(turned_ref[g], moved[:, HD:].astype(bf16)) * scale
            old = max_ref[g]
            top = jnp.maximum(old, jnp.max(score, 1, keepdims=True))
            shrink = jnp.exp2(old - top)
            expo = jnp.exp2(score - top)
            max_ref[g] = top
            sum_ref[g] = sum_ref[g] * shrink + expo
            acc_ref[g] = acc_ref[g] * shrink + dot(expo.astype(bf16), vals[block, :, lanes(g)])

    loop(0, me, absorb)

    pieces = []
    for g in span:
        total = jnp.sum(sum_ref[g], 1, keepdims=True)
        mean = (acc_ref[g] / total).astype(bf16)
        pieces += [mean[i * tok:(i + 1) * tok] for i in range(per_group)]
    attended = jnp.concatenate(pieces, 1)
    width = o_ref.shape[1]
    part = width // chunks

    def part_copy(dh, c):
        at = pl.ds(c * part, part)
        return pltpu.make_async_remote_copy(
            src_ref=part_out.at[dh - 1, :, at], dst_ref=part_in.at[dh - 1, :, at],
            send_sem=p_send.at[dh - 1, c], recv_sem=p_recv.at[dh - 1, c],
            device_id={"heads": lax.rem(head + dh, peers)}, device_id_type=MESH)

    for j in range(peers):
        copy_w(j).wait()
    for dh in range(1, peers):
        there = lax.rem(head + dh, peers)
        for c in range(chunks):
            at = pl.ds(pl.multiple_of(there * width + c * part, part), part)
            part_out[dh - 1, :, c * part:(c + 1) * part] = dot(attended, w_ref[:, at]).astype(bf16)
            part_copy(dh, c).start()
    mine = []
    for c in range(chunks):
        at = pl.ds(pl.multiple_of(head * width + c * part, part), part)
        mine.append(dot(attended, w_ref[:, at]))
    for c in range(chunks):
        total = mine[c]
        for dh in range(1, peers):
            part_copy(dh, c).wait_recv()
            total = total + part_in[dh - 1, :, c * part:(c + 1) * part].astype(f32)
        o_ref[:, c * part:(c + 1) * part] = total.astype(o_ref.dtype)

    sent_all(v_ref, vals, v_send, v_send_row, v_rel, v_recv)
    sent_all(own, far, e_send, e_send_row, e_rel, e_recv)
    for dh in range(1, peers):
        for c in range(chunks):
            part_copy(dh, c).wait_send()


def per_device(n, peers, queries, keys, values, house, beta, out_weight):
    tok = queries.shape[0]
    groups = keys.shape[1] // HD
    per_group = queries.shape[1] // keys.shape[1]
    width = out_weight.shape[1] // peers
    cols = max(c for c in range(1, n + 1) if n % c == 0 and c * c <= n)
    rows = n // cols
    chunks = 2
    many = per_group * tok
    vmem = pl.BlockSpec(memory_space=pltpu.VMEM)
    dma = pltpu.SemaphoreType.DMA
    body = functools.partial(kernel, n, cols, peers, groups, per_group, chunks)
    return pl.pallas_call(
        body,
        out_shape=jax.ShapeDtypeStruct((tok, width), bf16),
        in_specs=[vmem] * 5 + [pl.BlockSpec(memory_space=pl.ANY)],
        out_specs=vmem,
        scratch_shapes=[
            pltpu.VMEM(out_weight.shape, bf16),
            pltpu.VMEM((groups * HD, HD + tok), bf16),
            pltpu.VMEM((n, groups * HD, HD + tok), bf16),
            pltpu.VMEM((n,) + values.shape, bf16),
            pltpu.VMEM((groups, many, HD), bf16),
            pltpu.VMEM((groups, HD, HD), f32),
            pltpu.VMEM((groups, many, tok), f32),
            pltpu.VMEM((groups, many, tok), f32),
            pltpu.VMEM((groups, many, HD), f32),
            pltpu.VMEM((peers - 1, tok, width), bf16),
            pltpu.VMEM((peers - 1, tok, width), bf16),
            dma((peers,)),
            dma((rows,)), dma((cols,)), dma((rows, cols)), dma((n,)),
            dma((rows,)), dma((cols,)), dma((rows, cols)), dma((n,)),
            dma((peers - 1, chunks)), dma((peers - 1, chunks)),
        ],
        compiler_params=pltpu.CompilerParams(
            collective_id=0, has_side_effects=True, vmem_limit_bytes=48 * 2**20
        ),
    )(queries, keys, values, house, beta, out_weight)


def solution(mesh):
    in_specs = (
        P(("dp", "seq"), "heads"),
        P(("dp", "seq"), "heads"),
        P(("dp", "seq"), "heads"),
        P(("dp", "seq"), "heads"),
        P("heads", ("dp", "seq")),
        P("heads", None),
    )
    out_specs = P(("dp", "seq"), "heads")
    body = functools.partial(per_device, mesh.shape["seq"], mesh.shape["heads"])
    return jax.shard_map(
        body, mesh=mesh, in_specs=in_specs, out_specs=out_specs, check_vma=False
    )
```

```python
import functools
import math

import jax
import jax.numpy as jnp
from jax import lax
from jax.experimental import pallas as pl
from jax.experimental.pallas import tpu as pltpu
from jax.sharding import PartitionSpec as P

HD = 128
norm_floor = 1e-06
masked_score = -1e30
MESH = pl.DeviceIdType.MESH
f32 = jnp.float32
bf16 = jnp.bfloat16


def split(a):
    hi = a.astype(bf16)
    return hi, (a - hi.astype(f32)).astype(bf16)


def dot(a, b):
    return jnp.dot(a, b, preferred_element_type=f32)


def dot_two(ah, al, b):
    return dot(jnp.concatenate([ah, al], 1), jnp.concatenate([b, b], 0))


def dot_three(ah, al, bh, bl):
    return dot_two(ah, al, bh) + dot(ah, bl)


def kernel(n, cols, peers, groups, per_group, chunks, *refs):
    (q_hbm, k_hbm, v_hbm, h_hbm, beta_hbm, w_hbm, o_ref,
     q_ref, k_ref, v_ref, h_ref, beta_ref, w_ref, ends, maps, far, passed, vals,
     turned_ref, prod_ref, row_map, max_ref, sum_ref, acc_ref, part_out, part_in,
     in_sem, w_sem, v_send, v_send_row, v_rel, v_recv, m_send, m_recv,
     e_send, e_send_row, e_rel, e_recv, p_send, p_recv) = refs
    rows = n // cols
    tok = q_ref.shape[0]
    me = lax.axis_index("seq")
    head = lax.axis_index("heads")
    z = lax.div(me, cols)
    x = lax.rem(me, cols)

    small = [pltpu.make_async_copy(source, target, in_sem.at[i]) for i, (source, target) in
             enumerate([(v_hbm, v_ref), (h_hbm, h_ref), (k_hbm, k_ref), (beta_hbm, beta_ref),
                        (q_hbm, q_ref)])]
    for copy in small:
        copy.start()

    def copy_w(j):
        width = w_ref.shape[1] // peers
        at = pl.ds(j * width, width)
        return pltpu.make_async_copy(w_hbm.at[:, at], w_ref.at[:, at], w_sem.at[j])

    for j in range(peers):
        copy_w(j).start()

    barrier = pltpu.get_barrier_semaphore()
    for dz in (1, rows - 1):
        there = lax.rem(z + dz, rows) * cols + x
        pl.semaphore_signal(barrier, inc=1, device_id={"seq": there}, device_id_type=MESH)
    for dx in range(1, cols):
        there = z * cols + lax.rem(x + dx, cols)
        pl.semaphore_signal(barrier, inc=1, device_id={"seq": there}, device_id_type=MESH)
    for dh in range(1, peers):
        there = lax.rem(head + dh, peers)
        pl.semaphore_signal(barrier, inc=1, device_id={"heads": there}, device_id_type=MESH)
    pl.semaphore_wait(barrier, cols + peers)

    def to_next(source, slots, send, recv, zr):
        return pltpu.make_async_remote_copy(
            src_ref=source, dst_ref=slots.at[zr * cols + x], send_sem=send.at[zr],
            recv_sem=recv.at[zr * cols + x],
            device_id={"seq": lax.rem(z + 1, rows) * cols + x}, device_id_type=MESH)

    def row_copy(source, slots, send, recv, x2, at):
        return pltpu.make_async_remote_copy(
            src_ref=source, dst_ref=slots.at[at], send_sem=send.at[x2], recv_sem=recv.at[at],
            device_id={"seq": z * cols + x2}, device_id_type=MESH)

    def relay_copy(slots, send, recv, zr, dx):
        block = zr * cols + x
        return pltpu.make_async_remote_copy(
            src_ref=slots.at[block], dst_ref=slots.at[block], send_sem=send.at[zr, dx],
            recv_sem=recv.at[block],
            device_id={"seq": z * cols + lax.rem(x + dx, cols)}, device_id_type=MESH)

    def wait_block(slots, recv, block):
        pltpu.make_async_remote_copy(
            src_ref=slots.at[block], dst_ref=slots.at[block], send_sem=w_sem.at[0],
            recv_sem=recv.at[block], device_id={"heads": lax.rem(head + 1, peers)},
            device_id_type=MESH).wait_recv()

    def loop(lower, upper, body):
        def step(i, carry):
            body(i)
            return carry
        lax.fori_loop(lower, upper, step, 0)

    more = z + 1 < rows

    def row_maps(body):
        for dx in range(1, cols):
            body(row_copy(maps.at[x], maps, m_send, m_recv, lax.rem(x + dx, cols), x))

    def relay_values(zr):
        wait_block(vals, v_recv, zr * cols + x)

        @pl.when(more)
        def _():
            to_next(vals.at[zr * cols + x], vals, v_send, v_recv, zr).start()
        for dx in range(1, cols):
            relay_copy(vals, v_rel, v_recv, zr, dx).start()

    def relay_values_at(step):
        @pl.when(z - step >= 0)
        def _():
            relay_values(z - step)

    small[0].wait()

    @pl.when(more)
    def _():
        to_next(v_ref, vals, v_send, v_recv, z).start()
    loop(x + 1, cols,
         lambda x2: row_copy(v_ref, vals, v_send_row, v_recv, x2, me).start())
    for copy in small[1:]:
        copy.wait()

    row = lax.broadcasted_iota(jnp.int32, (tok, tok), 0)
    col = lax.broadcasted_iota(jnp.int32, (tok, tok), 1)
    diag = row == col
    eye = diag.astype(f32)
    below = col < row
    differ = row ^ col
    upto = jnp.concatenate([col <= row] * per_group, 0)
    scale = math.log2(math.e) / math.sqrt(HD)
    span = range(groups)

    def lanes(g):
        return slice(g * HD, (g + 1) * HD)

    h = [h_ref[:, lanes(g)] for g in span]
    k = [k_ref[:, lanes(g)] for g in span]
    q = [jnp.concatenate([q_ref[:, lanes(g * per_group + i)] for i in range(per_group)], 0)
         for g in span]
    h_t = [h[g].T for g in span]
    k_t = [k[g].T for g in span]
    hk_t = [jnp.concatenate([h_t[g], k_t[g]], 1) for g in span]
    first = [dot(h[g], hk_t[g]) for g in span]
    gram = [first[g][:, :tok] for g in span]
    square = [jnp.where(diag, gram[g], 0.0) for g in span]
    s_col = [lax.rsqrt(jnp.sum(square[g], 1, keepdims=True) + norm_floor) for g in span]
    s_row = [lax.rsqrt(jnp.sum(square[g], 0, keepdims=True) + norm_floor) for g in span]
    beta_row = [beta_ref[g:g + 1, :] for g in span]
    beta_col = [jnp.sum(jnp.where(diag, beta_row[g], 0.0), 1, keepdims=True) for g in span]
    strict = [jnp.where(below, gram[g] * (s_col[g] * beta_col[g]) * s_row[g], 0.0) for g in span]
    key_along = [jnp.where(below, first[g][:, tok:] * s_col[g], 0.0) for g in span]
    parts = [split(strict[g]) for g in span]
    inverse = [eye - jnp.where(differ == 1, strict[g], 0.0) for g in span]
    size = 2
    stage = 0
    while size < tok:
        mask = (differ >= size) & (differ < 2 * size)
        halves = [split(inverse[g]) for g in span]
        zero = jnp.zeros((tok, tok), bf16)
        inner = [dot_three(jnp.where(mask, parts[g][0], zero), jnp.where(mask, parts[g][1], zero),
                           *halves[g]) for g in span]
        inner = [split(inner[g]) for g in span]
        inverse = [inverse[g] - dot_three(*halves[g], *inner[g]) for g in span]
        if size in (tok // 16, tok // 4):
            stage += 1
            relay_values_at(stage)
        size *= 2
    solver = [split(inverse[g] * beta_row[g]) for g in span]
    right = [split(jnp.concatenate([h[g].astype(f32) * s_col[g], key_along[g]], 1)) for g in span]
    solved = [dot_three(*solver[g], *right[g]) for g in span]
    scaled = [split(solved[g] * s_col[g]) for g in span]
    for g in span:
        base = jnp.concatenate([eye, k_t[g].astype(f32)], 1)
        turn = dot(jnp.concatenate([h_t[g], h_t[g]], 1), jnp.concatenate(scaled[g], 0))
        made = (base - turn).astype(bf16)
        maps[x, g * HD:(g + 1) * HD, :] = made[:, :HD]
        ends[g * HD:(g + 1) * HD, :] = made[:, HD:]
    row_maps(lambda copy: copy.start())

    @pl.when(more & (x == cols - 1))
    def _():
        to_next(ends, far, e_send, e_recv, z).start()
    loop(x + 1, cols,
         lambda x2: row_copy(ends, far, e_send_row, e_recv, x2, me).start())

    def own_scores(g):
        second = dot(q[g], hk_t[g])
        along = split(jnp.where(upto, second[:, :tok] * s_row[g], 0.0))
        base = jnp.concatenate([q[g].astype(f32), second[:, tok:]], 1)
        both = base - dot_three(*along, *split(solved[g]))
        turned_ref[g] = both[:, :HD].astype(bf16)
        score = jnp.where(upto, both[:, HD:] * scale, masked_score)
        top = jnp.max(score, 1, keepdims=True)
        expo = jnp.exp2(score - top)
        max_ref[g] = jnp.broadcast_to(top, max_ref.shape[1:])
        sum_ref[g] = expo
        acc_ref[g] = dot(expo.astype(bf16), v_ref[:, lanes(g)])
        prod_ref[g] = eye
        row_map[g] = eye

    def under(g):
        return slice(g * HD, (g + 1) * HD)

    def map_times(block_map, value):
        return dot(jnp.concatenate([block_map, block_map], 1), jnp.concatenate(split(value), 0))

    for g in range(0, groups, 2):
        own_scores(g)

    for dx in range(1, cols):
        wait_block(maps, m_recv, lax.rem(x + dx, cols))

    @pl.when(more & (x < cols - 1))
    def _():
        for g in span:
            def move(xr, value):
                return map_times(maps[xr, under(g), :], value)
            value = lax.fori_loop(x + 1, cols, move, ends[under(g), :].astype(f32))
            passed[z, under(g), :] = value.astype(bf16)
        to_next(passed.at[z], far, e_send, e_recv, z).start()

    for g in range(1, groups, 2):
        own_scores(g)
    for g in span:
        value = maps[0, under(g), :].astype(f32)
        for xr in range(1, cols):
            value = map_times(maps[xr, under(g), :], value)
        row_map[g] = value

    for step in range(stage + 1, rows):
        relay_values_at(step)

    def relay_keys(zr):
        block = zr * cols + x
        wait_block(far, e_recv, block)
        for dx in range(1, cols):
            relay_copy(far, e_rel, e_recv, zr, dx).start()

        @pl.when(more)
        def _():
            for g in span:
                moved = dot_two(*split(row_map[g]), far[block, under(g), :])
                passed[zr, under(g), :] = moved.astype(bf16)
            to_next(passed.at[zr], far, e_send, e_recv, zr).start()

    def absorb(i):
        block = me - 1 - i
        zr = lax.div(block, cols)
        xr = lax.rem(block, cols)
        earlier = zr < z

        @pl.when(earlier & (xr == cols - 1))
        def _():
            relay_keys(zr)

        @pl.when(jnp.logical_not(earlier & (xr == x)))
        def _():
            wait_block(vals, v_recv, block)
            wait_block(far, e_recv, block)

        for g in span:
            moved = dot_two(*split(prod_ref[g]), far[block, under(g), :])
            score = dot(turned_ref[g], moved.astype(bf16)) * scale
            old = max_ref[g]
            top = jnp.maximum(old, jnp.max(score, 1, keepdims=True))
            shrink = jnp.exp2(old - top)
            expo = jnp.exp2(score - top)
            max_ref[g] = top
            sum_ref[g] = sum_ref[g] * shrink + expo
            acc_ref[g] = acc_ref[g] * shrink + dot(expo.astype(bf16), vals[block, :, lanes(g)])

        @pl.when(jnp.logical_not(earlier))
        def _():
            for g in span:
                prod_ref[g] = dot_two(*split(prod_ref[g]), maps[xr, under(g), :])

    loop(0, me, absorb)

    pieces = []
    for g in span:
        total = jnp.sum(sum_ref[g], 1, keepdims=True)
        mean = (acc_ref[g] / total).astype(bf16)
        pieces += [mean[i * tok:(i + 1) * tok] for i in range(per_group)]
    attended = jnp.concatenate(pieces, 1)
    width = o_ref.shape[1]
    part = width // chunks

    def part_copy(dh, c):
        at = pl.ds(c * part, part)
        return pltpu.make_async_remote_copy(
            src_ref=part_out.at[dh - 1, :, at], dst_ref=part_in.at[dh - 1, :, at],
            send_sem=p_send.at[dh - 1, c], recv_sem=p_recv.at[dh - 1, c],
            device_id={"heads": lax.rem(head + dh, peers)}, device_id_type=MESH)

    for j in range(peers):
        copy_w(j).wait()
    for dh in range(1, peers):
        there = lax.rem(head + dh, peers)
        for c in range(chunks):
            at = pl.ds(pl.multiple_of(there * width + c * part, part), part)
            part_out[dh - 1, :, c * part:(c + 1) * part] = dot(attended, w_ref[:, at]).astype(bf16)
            part_copy(dh, c).start()
    mine = []
    for c in range(chunks):
        at = pl.ds(pl.multiple_of(head * width + c * part, part), part)
        mine.append(dot(attended, w_ref[:, at]))
    for c in range(chunks):
        total = mine[c]
        for dh in range(1, peers):
            part_copy(dh, c).wait_recv()
            total = total + part_in[dh - 1, :, c * part:(c + 1) * part].astype(f32)
        o_ref[:, c * part:(c + 1) * part] = total.astype(o_ref.dtype)

    row_maps(lambda copy: copy.wait_send())
    loop(x + 1, cols,
         lambda x2: row_copy(v_ref, vals, v_send_row, v_recv, x2, me).wait_send())
    loop(x + 1, cols,
         lambda x2: row_copy(ends, far, e_send_row, e_recv, x2, me).wait_send())

    def relayed(zr):
        for dx in range(1, cols):
            relay_copy(vals, v_rel, v_recv, zr, dx).wait_send()
            relay_copy(far, e_rel, e_recv, zr, dx).wait_send()
    loop(0, z, relayed)

    def handed(zr):
        to_next(passed.at[zr], far, e_send, e_recv, zr).wait_send()
        to_next(v_ref, vals, v_send, v_recv, zr).wait_send()

    @pl.when(more)
    def _():
        loop(0, z + 1, handed)
    for dh in range(1, peers):
        for c in range(chunks):
            part_copy(dh, c).wait_send()


def per_device(n, peers, queries, keys, values, house, beta, out_weight):
    tok = queries.shape[0]
    groups = keys.shape[1] // HD
    per_group = queries.shape[1] // keys.shape[1]
    width = out_weight.shape[1] // peers
    cols = max(c for c in range(1, n + 1) if n % c == 0 and c * c <= n)
    rows = n // cols
    chunks = 2
    many = per_group * tok
    vmem = pl.BlockSpec(memory_space=pltpu.VMEM)
    hbm = pl.BlockSpec(memory_space=pltpu.HBM)
    dma = pltpu.SemaphoreType.DMA
    body = functools.partial(kernel, n, cols, peers, groups, per_group, chunks)
    inputs = (queries, keys, values, house, beta, out_weight)
    return pl.pallas_call(
        body,
        out_shape=jax.ShapeDtypeStruct((tok, width), bf16),
        in_specs=[hbm] * len(inputs),
        out_specs=vmem,
        scratch_shapes=[pltpu.VMEM(one.shape, one.dtype) for one in inputs] + [
            pltpu.VMEM((groups * HD, tok), bf16),
            pltpu.VMEM((cols, groups * HD, HD), bf16),
            pltpu.VMEM((n, groups * HD, tok), bf16),
            pltpu.VMEM((rows, groups * HD, tok), bf16),
            pltpu.VMEM((n,) + values.shape, bf16),
            pltpu.VMEM((groups, many, HD), bf16),
            pltpu.VMEM((groups, HD, HD), f32),
            pltpu.VMEM((groups, HD, HD), f32),
            pltpu.VMEM((groups, many, tok), f32),
            pltpu.VMEM((groups, many, tok), f32),
            pltpu.VMEM((groups, many, HD), f32),
            pltpu.VMEM((peers - 1, tok, width), bf16),
            pltpu.VMEM((peers - 1, tok, width), bf16),
            dma((len(inputs) - 1,)), dma((peers,)),
            dma((rows,)), dma((cols,)), dma((rows, cols)), dma((n,)),
            dma((cols,)), dma((cols,)),
            dma((rows,)), dma((cols,)), dma((rows, cols)), dma((n,)),
            dma((peers - 1, chunks)), dma((peers - 1, chunks)),
        ],
        compiler_params=pltpu.CompilerParams(
            collective_id=0, has_side_effects=True, vmem_limit_bytes=63 * 2**20
        ),
    )(*inputs)


def solution(mesh):
    in_specs = (
        P(("dp", "seq"), "heads"),
        P(("dp", "seq"), "heads"),
        P(("dp", "seq"), "heads"),
        P(("dp", "seq"), "heads"),
        P("heads", ("dp", "seq")),
        P("heads", None),
    )
    out_specs = P(("dp", "seq"), "heads")
    body = functools.partial(per_device, mesh.shape["seq"], mesh.shape["heads"])
    return jax.shard_map(
        body, mesh=mesh, in_specs=in_specs, out_specs=out_specs, check_vma=False
    )
```

```python
import functools
import math

import jax
import jax.numpy as jnp
from jax import lax
from jax.experimental import pallas as pl
from jax.experimental.pallas import tpu as pltpu
from jax.sharding import PartitionSpec as P

HD = 128
norm_floor = 1e-06
masked_score = -1e30
MESH = pl.DeviceIdType.MESH
f32 = jnp.float32
bf16 = jnp.bfloat16


def split(a):
    hi = a.astype(bf16)
    return hi, (a - hi.astype(f32)).astype(bf16)


def dot(a, b):
    return jnp.dot(a, b, preferred_element_type=f32)


def dot_two(ah, al, b):
    return dot(jnp.concatenate([ah, al], 1), jnp.concatenate([b, b], 0))


def dot_three(ah, al, bh, bl):
    return dot_two(ah, al, bh) + dot(ah, bl)


def kernel(n, cols, peers, groups, per_group, chunks, *refs):
    (q_hbm, k_hbm, v_hbm, h_hbm, beta_hbm, w_hbm, o_ref,
     q_ref, k_ref, v_ref, h_ref, beta_ref, w_ref, ends, maps, far, passed, vals,
     turned_ref, prod_ref, row_map, max_ref, sum_ref, acc_ref, part_out, part_in,
     in_sem, w_sem, v_send, v_send_row, v_rel, v_recv, m_send, m_recv,
     e_send, e_send_row, e_rel, e_recv, p_send, p_recv) = refs
    rows = n // cols
    tok = q_ref.shape[0]
    me = lax.axis_index("seq")
    head = lax.axis_index("heads")
    z = lax.div(me, cols)
    x = lax.rem(me, cols)

    small = [pltpu.make_async_copy(source, target, in_sem.at[i]) for i, (source, target) in
             enumerate([(v_hbm, v_ref), (h_hbm, h_ref), (k_hbm, k_ref), (beta_hbm, beta_ref),
                        (q_hbm, q_ref)])]
    for copy in small:
        copy.start()

    def copy_w(j):
        width = w_ref.shape[1] // peers
        at = pl.ds(j * width, width)
        return pltpu.make_async_copy(w_hbm.at[:, at], w_ref.at[:, at], w_sem.at[j])

    for j in range(peers):
        copy_w(j).start()

    barrier = pltpu.get_barrier_semaphore()
    for dz in (1, rows - 1):
        there = lax.rem(z + dz, rows) * cols + x
        pl.semaphore_signal(barrier, inc=1, device_id={"seq": there}, device_id_type=MESH)
    for dx in range(1, cols):
        there = z * cols + lax.rem(x + dx, cols)
        pl.semaphore_signal(barrier, inc=1, device_id={"seq": there}, device_id_type=MESH)
    for dh in range(1, peers):
        there = lax.rem(head + dh, peers)
        pl.semaphore_signal(barrier, inc=1, device_id={"heads": there}, device_id_type=MESH)
    pl.semaphore_wait(barrier, cols + peers)

    def to_next(source, slots, send, recv, zr):
        return pltpu.make_async_remote_copy(
            src_ref=source, dst_ref=slots.at[zr * cols + x], send_sem=send.at[zr],
            recv_sem=recv.at[zr * cols + x],
            device_id={"seq": lax.rem(z + 1, rows) * cols + x}, device_id_type=MESH)

    def row_copy(source, slots, send, recv, x2, at):
        return pltpu.make_async_remote_copy(
            src_ref=source, dst_ref=slots.at[at], send_sem=send.at[x2], recv_sem=recv.at[at],
            device_id={"seq": z * cols + x2}, device_id_type=MESH)

    def relay_copy(slots, send, recv, zr, dx):
        block = zr * cols + x
        return pltpu.make_async_remote_copy(
            src_ref=slots.at[block], dst_ref=slots.at[block], send_sem=send.at[zr, dx],
            recv_sem=recv.at[block],
            device_id={"seq": z * cols + lax.rem(x + dx, cols)}, device_id_type=MESH)

    def wait_block(slots, recv, block):
        pltpu.make_async_remote_copy(
            src_ref=slots.at[block], dst_ref=slots.at[block], send_sem=w_sem.at[0],
            recv_sem=recv.at[block], device_id={"heads": lax.rem(head + 1, peers)},
            device_id_type=MESH).wait_recv()

    def loop(lower, upper, body):
        def step(i, carry):
            body(i)
            return carry
        lax.fori_loop(lower, upper, step, 0)

    more = z + 1 < rows

    def row_maps(body):
        for dx in range(1, cols):
            body(row_copy(maps.at[x], maps, m_send, m_recv, lax.rem(x + dx, cols), x))

    def relay_values(zr):
        wait_block(vals, v_recv, zr * cols + x)

        @pl.when(more)
        def _():
            to_next(vals.at[zr * cols + x], vals, v_send, v_recv, zr).start()
        for dx in range(1, cols):
            relay_copy(vals, v_rel, v_recv, zr, dx).start()

    def relay_values_at(step):
        @pl.when(z - step >= 0)
        def _():
            relay_values(z - step)

    small[0].wait()

    @pl.when(more)
    def _():
        to_next(v_ref, vals, v_send, v_recv, z).start()
    loop(x + 1, cols,
         lambda x2: row_copy(v_ref, vals, v_send_row, v_recv, x2, me).start())
    for copy in small[1:]:
        copy.wait()

    row = lax.broadcasted_iota(jnp.int32, (tok, tok), 0)
    col = lax.broadcasted_iota(jnp.int32, (tok, tok), 1)
    diag = row == col
    eye = diag.astype(f32)
    below = col < row
    differ = row ^ col
    upto = jnp.concatenate([col <= row] * per_group, 0)
    scale = math.log2(math.e) / math.sqrt(HD)
    span = range(groups)

    def lanes(g):
        return slice(g * HD, (g + 1) * HD)

    h = [h_ref[:, lanes(g)] for g in span]
    k = [k_ref[:, lanes(g)] for g in span]
    q = [jnp.concatenate([q_ref[:, lanes(g * per_group + i)] for i in range(per_group)], 0)
         for g in span]
    h_t = [h[g].T for g in span]
    k_t = [k[g].T for g in span]
    hk_t = [jnp.concatenate([h_t[g], k_t[g]], 1) for g in span]
    first = [dot(h[g], hk_t[g]) for g in span]
    gram = [first[g][:, :tok] for g in span]
    square = [jnp.where(diag, gram[g], 0.0) for g in span]
    s_col = [lax.rsqrt(jnp.sum(square[g], 1, keepdims=True) + norm_floor) for g in span]
    s_row = [lax.rsqrt(jnp.sum(square[g], 0, keepdims=True) + norm_floor) for g in span]
    beta_row = [beta_ref[g:g + 1, :] for g in span]
    beta_col = [jnp.sum(jnp.where(diag, beta_row[g], 0.0), 1, keepdims=True) for g in span]
    strict = [jnp.where(below, gram[g] * (s_col[g] * beta_col[g]) * s_row[g], 0.0) for g in span]
    key_along = [jnp.where(below, first[g][:, tok:] * s_col[g], 0.0) for g in span]
    parts = [split(strict[g]) for g in span]
    inverse = [eye - jnp.where(differ == 1, strict[g], 0.0) for g in span]
    size = 2
    stage = 0
    while size < tok:
        mask = (differ >= size) & (differ < 2 * size)
        halves = [split(inverse[g]) for g in span]
        zero = jnp.zeros((tok, tok), bf16)
        inner = [dot_three(jnp.where(mask, parts[g][0], zero), jnp.where(mask, parts[g][1], zero),
                           *halves[g]) for g in span]
        inner = [split(inner[g]) for g in span]
        inverse = [inverse[g] - dot_three(*halves[g], *inner[g]) for g in span]
        if size in (tok // 16, tok // 4):
            stage += 1
            relay_values_at(stage)
        size *= 2
    solver = [split(inverse[g] * beta_row[g]) for g in span]
    right = [split(jnp.concatenate([h[g].astype(f32) * s_col[g], key_along[g]], 1)) for g in span]
    solved = [dot_three(*solver[g], *right[g]) for g in span]
    scaled = [split(solved[g] * s_col[g]) for g in span]
    for g in span:
        base = jnp.concatenate([eye, k_t[g].astype(f32)], 1)
        turn = dot(jnp.concatenate([h_t[g], h_t[g]], 1), jnp.concatenate(scaled[g], 0))
        made = (base - turn).astype(bf16)
        maps[x, g * HD:(g + 1) * HD, :] = made[:, :HD]
        ends[g * HD:(g + 1) * HD, :] = made[:, HD:]
    row_maps(lambda copy: copy.start())

    @pl.when(more & (x == cols - 1))
    def _():
        to_next(ends, far, e_send, e_recv, z).start()
    loop(x + 1, cols,
         lambda x2: row_copy(ends, far, e_send_row, e_recv, x2, me).start())

    def own_scores(g):
        second = dot(q[g], hk_t[g])
        along = split(jnp.where(upto, second[:, :tok] * s_row[g], 0.0))
        base = jnp.concatenate([q[g].astype(f32), second[:, tok:]], 1)
        both = base - dot_three(*along, *split(solved[g]))
        turned_ref[g] = both[:, :HD].astype(bf16)
        score = jnp.where(upto, both[:, HD:] * scale, masked_score)
        top = jnp.max(score, 1, keepdims=True)
        expo = jnp.exp2(score - top)
        max_ref[g] = jnp.broadcast_to(top, max_ref.shape[1:])
        sum_ref[g] = expo
        acc_ref[g] = dot(expo.astype(bf16), v_ref[:, lanes(g)])
        prod_ref[g] = eye
        row_map[g] = eye

    def under(g):
        return slice(g * HD, (g + 1) * HD)

    def map_times(block_map, value):
        return dot(jnp.concatenate([block_map, block_map], 1), jnp.concatenate(split(value), 0))

    for g in range(0, groups, 2):
        own_scores(g)

    for dx in range(1, cols):
        wait_block(maps, m_recv, lax.rem(x + dx, cols))

    @pl.when(more & (x < cols - 1))
    def _():
        for g in span:
            def move(xr, value):
                return map_times(maps[xr, under(g), :], value)
            value = lax.fori_loop(x + 1, cols, move, ends[under(g), :].astype(f32))
            passed[z, under(g), :] = value.astype(bf16)
        to_next(passed.at[z], far, e_send, e_recv, z).start()

    for g in range(1, groups, 2):
        own_scores(g)
    for g in span:
        value = maps[0, under(g), :].astype(f32)
        for xr in range(1, cols):
            value = map_times(maps[xr, under(g), :], value)
        row_map[g] = value

    for step in range(stage + 1, rows):
        relay_values_at(step)

    def relay_keys(zr):
        block = zr * cols + x
        wait_block(far, e_recv, block)
        for dx in range(1, cols):
            relay_copy(far, e_rel, e_recv, zr, dx).start()

        @pl.when(more)
        def _():
            for g in span:
                moved = dot_two(*split(row_map[g]), far[block, under(g), :])
                passed[zr, under(g), :] = moved.astype(bf16)
            to_next(passed.at[zr], far, e_send, e_recv, zr).start()

    def absorb(block):
        for g in span:
            moved = dot_two(*split(prod_ref[g]), far[block, under(g), :])
            score = dot(turned_ref[g], moved.astype(bf16)) * scale
            old = max_ref[g]
            top = jnp.maximum(old, jnp.max(score, 1, keepdims=True))
            shrink = jnp.exp2(old - top)
            expo = jnp.exp2(score - top)
            max_ref[g] = top
            sum_ref[g] = sum_ref[g] * shrink + expo
            acc_ref[g] = acc_ref[g] * shrink + dot(expo.astype(bf16), vals[block, :, lanes(g)])

    def same_row(i):
        xr = x - 1 - i
        wait_block(vals, v_recv, z * cols + xr)
        wait_block(far, e_recv, z * cols + xr)
        absorb(z * cols + xr)
        for g in span:
            prod_ref[g] = dot_two(*split(prod_ref[g]), maps[xr, under(g), :])

    def earlier_row(i):
        zr = z - 1 - i

        def one(j):
            block = zr * cols + lax.rem(x + j, cols)

            @pl.when(j == min(1, cols - 1))
            def _():
                @pl.when(zr > 0)
                def _():
                    relay_keys(zr - 1)

            @pl.when(j > 0)
            def _():
                wait_block(vals, v_recv, block)
                wait_block(far, e_recv, block)
            absorb(block)
        loop(0, cols, one)

    @pl.when(z > 0)
    def _():
        relay_keys(z - 1)
    loop(0, x, same_row)
    loop(0, z, earlier_row)

    pieces = []
    for g in span:
        total = jnp.sum(sum_ref[g], 1, keepdims=True)
        mean = (acc_ref[g] / total).astype(bf16)
        pieces += [mean[i * tok:(i + 1) * tok] for i in range(per_group)]
    attended = jnp.concatenate(pieces, 1)
    width = o_ref.shape[1]
    part = width // chunks

    def part_copy(dh, c):
        at = pl.ds(c * part, part)
        return pltpu.make_async_remote_copy(
            src_ref=part_out.at[dh - 1, :, at], dst_ref=part_in.at[dh - 1, :, at],
            send_sem=p_send.at[dh - 1, c], recv_sem=p_recv.at[dh - 1, c],
            device_id={"heads": lax.rem(head + dh, peers)}, device_id_type=MESH)

    for j in range(peers):
        copy_w(j).wait()
    for dh in range(1, peers):
        there = lax.rem(head + dh, peers)
        for c in range(chunks):
            at = pl.ds(pl.multiple_of(there * width + c * part, part), part)
            part_out[dh - 1, :, c * part:(c + 1) * part] = dot(attended, w_ref[:, at]).astype(bf16)
            part_copy(dh, c).start()
    mine = []
    for c in range(chunks):
        at = pl.ds(pl.multiple_of(head * width + c * part, part), part)
        mine.append(dot(attended, w_ref[:, at]))
    for c in range(chunks):
        total = mine[c]
        for dh in range(1, peers):
            part_copy(dh, c).wait_recv()
            total = total + part_in[dh - 1, :, c * part:(c + 1) * part].astype(f32)
        o_ref[:, c * part:(c + 1) * part] = total.astype(o_ref.dtype)

    row_maps(lambda copy: copy.wait_send())
    loop(x + 1, cols,
         lambda x2: row_copy(v_ref, vals, v_send_row, v_recv, x2, me).wait_send())
    loop(x + 1, cols,
         lambda x2: row_copy(ends, far, e_send_row, e_recv, x2, me).wait_send())

    def relayed(zr):
        for dx in range(1, cols):
            relay_copy(vals, v_rel, v_recv, zr, dx).wait_send()
            relay_copy(far, e_rel, e_recv, zr, dx).wait_send()
    loop(0, z, relayed)

    def handed(zr):
        to_next(passed.at[zr], far, e_send, e_recv, zr).wait_send()
        to_next(v_ref, vals, v_send, v_recv, zr).wait_send()

    @pl.when(more)
    def _():
        loop(0, z + 1, handed)
    for dh in range(1, peers):
        for c in range(chunks):
            part_copy(dh, c).wait_send()


def per_device(n, peers, queries, keys, values, house, beta, out_weight):
    tok = queries.shape[0]
    groups = keys.shape[1] // HD
    per_group = queries.shape[1] // keys.shape[1]
    width = out_weight.shape[1] // peers
    cols = max(c for c in range(1, n + 1) if n % c == 0 and c * c <= n)
    rows = n // cols
    chunks = 2
    many = per_group * tok
    vmem = pl.BlockSpec(memory_space=pltpu.VMEM)
    hbm = pl.BlockSpec(memory_space=pltpu.HBM)
    dma = pltpu.SemaphoreType.DMA
    body = functools.partial(kernel, n, cols, peers, groups, per_group, chunks)
    inputs = (queries, keys, values, house, beta, out_weight)
    return pl.pallas_call(
        body,
        out_shape=jax.ShapeDtypeStruct((tok, width), f32),
        in_specs=[hbm] * len(inputs),
        out_specs=vmem,
        scratch_shapes=[pltpu.VMEM(one.shape, one.dtype) for one in inputs] + [
            pltpu.VMEM((groups * HD, tok), bf16),
            pltpu.VMEM((cols, groups * HD, HD), bf16),
            pltpu.VMEM((n, groups * HD, tok), bf16),
            pltpu.VMEM((rows, groups * HD, tok), bf16),
            pltpu.VMEM((n,) + values.shape, bf16),
            pltpu.VMEM((groups, many, HD), bf16),
            pltpu.VMEM((groups, HD, HD), f32),
            pltpu.VMEM((groups, HD, HD), f32),
            pltpu.VMEM((groups, many, tok), f32),
            pltpu.VMEM((groups, many, tok), f32),
            pltpu.VMEM((groups, many, HD), f32),
            pltpu.VMEM((peers - 1, tok, width), bf16),
            pltpu.VMEM((peers - 1, tok, width), bf16),
            dma((len(inputs) - 1,)), dma((peers,)),
            dma((rows,)), dma((cols,)), dma((rows, cols)), dma((n,)),
            dma((cols,)), dma((cols,)),
            dma((rows,)), dma((cols,)), dma((rows, cols)), dma((n,)),
            dma((peers - 1, chunks)), dma((peers - 1, chunks)),
        ],
        compiler_params=pltpu.CompilerParams(
            collective_id=0, has_side_effects=True, vmem_limit_bytes=63 * 2**20
        ),
    )(*inputs).astype(bf16)


def solution(mesh):
    in_specs = (
        P(("dp", "seq"), "heads"),
        P(("dp", "seq"), "heads"),
        P(("dp", "seq"), "heads"),
        P(("dp", "seq"), "heads"),
        P("heads", ("dp", "seq")),
        P("heads", None),
    )
    out_specs = P(("dp", "seq"), "heads")
    body = functools.partial(per_device, mesh.shape["seq"], mesh.shape["heads"])
    return jax.shard_map(
        body, mesh=mesh, in_specs=in_specs, out_specs=out_specs, check_vma=False
    )
```

```python
import functools
import math

import jax
import jax.numpy as jnp
from jax import lax
from jax.experimental import pallas as pl
from jax.experimental.pallas import tpu as pltpu
from jax.sharding import PartitionSpec as P

HD = 128
norm_floor = 1e-06
masked_score = -1e30
MESH = pl.DeviceIdType.MESH
f32 = jnp.float32
bf16 = jnp.bfloat16


def split(a):
    hi = a.astype(bf16)
    return hi, (a - hi.astype(f32)).astype(bf16)


def dot(a, b):
    return jnp.dot(a, b, preferred_element_type=f32)


def dot_two(ah, al, b):
    return dot(jnp.concatenate([ah, al], 1), jnp.concatenate([b, b], 0))


def dot_three(ah, al, bh, bl):
    return dot_two(ah, al, bh) + dot(ah, bl)


def kernel(n, cols, peers, groups, per_group, chunks, *refs):
    (q_hbm, k_hbm, v_hbm, h_hbm, beta_hbm, w_hbm, o_ref,
     q_ref, k_ref, v_ref, h_ref, beta_ref, w_ref, ends, maps, far, passed, vals,
     turned_ref, prod_ref, row_map, max_ref, sum_ref, acc_ref, part_out, part_in,
     in_sem, w_sem, v_send, v_send_row, v_rel, v_recv, m_send, m_recv,
     e_send, e_send_row, e_rel, e_recv, p_send, p_recv) = refs
    rows = n // cols
    tok = q_ref.shape[0]
    me = lax.axis_index("seq")
    head = lax.axis_index("heads")
    z = lax.div(me, cols)
    x = lax.rem(me, cols)

    small = [pltpu.make_async_copy(source, target, in_sem.at[i]) for i, (source, target) in
             enumerate([(v_hbm, v_ref), (h_hbm, h_ref), (k_hbm, k_ref), (beta_hbm, beta_ref),
                        (q_hbm, q_ref)])]
    for copy in small:
        copy.start()

    def copy_w(j):
        width = w_ref.shape[1] // peers
        at = pl.ds(j * width, width)
        return pltpu.make_async_copy(w_hbm.at[:, at], w_ref.at[:, at], w_sem.at[j])

    for j in range(peers):
        copy_w(j).start()

    barrier = pltpu.get_barrier_semaphore()
    for dz in (1, rows - 1):
        there = lax.rem(z + dz, rows) * cols + x
        pl.semaphore_signal(barrier, inc=1, device_id={"seq": there}, device_id_type=MESH)
    for dx in range(1, cols):
        there = z * cols + lax.rem(x + dx, cols)
        pl.semaphore_signal(barrier, inc=1, device_id={"seq": there}, device_id_type=MESH)
    for dh in range(1, peers):
        there = lax.rem(head + dh, peers)
        pl.semaphore_signal(barrier, inc=1, device_id={"heads": there}, device_id_type=MESH)
    pl.semaphore_wait(barrier, cols + peers)

    def to_next(source, slots, send, recv, zr):
        return pltpu.make_async_remote_copy(
            src_ref=source, dst_ref=slots.at[zr * cols + x], send_sem=send.at[zr],
            recv_sem=recv.at[zr * cols + x],
            device_id={"seq": lax.rem(z + 1, rows) * cols + x}, device_id_type=MESH)

    def row_copy(source, slots, send, recv, x2, at):
        return pltpu.make_async_remote_copy(
            src_ref=source, dst_ref=slots.at[at], send_sem=send.at[x2], recv_sem=recv.at[at],
            device_id={"seq": z * cols + x2}, device_id_type=MESH)

    def relay_copy(slots, send, recv, zr, dx):
        block = zr * cols + x
        return pltpu.make_async_remote_copy(
            src_ref=slots.at[block], dst_ref=slots.at[block], send_sem=send.at[zr, dx],
            recv_sem=recv.at[block],
            device_id={"seq": z * cols + lax.rem(x + dx, cols)}, device_id_type=MESH)

    def wait_block(slots, recv, block):
        pltpu.make_async_remote_copy(
            src_ref=slots.at[block], dst_ref=slots.at[block], send_sem=w_sem.at[0],
            recv_sem=recv.at[block], device_id={"heads": lax.rem(head + 1, peers)},
            device_id_type=MESH).wait_recv()

    def loop(lower, upper, body):
        def step(i, carry):
            body(i)
            return carry
        lax.fori_loop(lower, upper, step, 0)

    more = z + 1 < rows

    def row_maps(body):
        for dx in range(1, cols):
            body(row_copy(maps.at[x], maps, m_send, m_recv, lax.rem(x + dx, cols), x))

    def relay_values(zr):
        wait_block(vals, v_recv, zr * cols + x)

        @pl.when(more)
        def _():
            to_next(vals.at[zr * cols + x], vals, v_send, v_recv, zr).start()
        for dx in range(1, cols):
            relay_copy(vals, v_rel, v_recv, zr, dx).start()

    def relay_values_at(step):
        @pl.when(z - step >= 0)
        def _():
            relay_values(z - step)

    small[0].wait()

    @pl.when(more)
    def _():
        to_next(v_ref, vals, v_send, v_recv, z).start()
    loop(x + 1, cols,
         lambda x2: row_copy(v_ref, vals, v_send_row, v_recv, x2, me).start())
    for copy in small[1:]:
        copy.wait()

    row = lax.broadcasted_iota(jnp.int32, (tok, tok), 0)
    col = lax.broadcasted_iota(jnp.int32, (tok, tok), 1)
    diag = row == col
    eye = diag.astype(f32)
    below = col < row
    differ = row ^ col
    upto = jnp.concatenate([col <= row] * per_group, 0)
    scale = math.log2(math.e) / math.sqrt(HD)
    span = range(groups)

    def lanes(g):
        return slice(g * HD, (g + 1) * HD)

    h = [h_ref[:, lanes(g)] for g in span]
    k = [k_ref[:, lanes(g)] for g in span]
    q = [jnp.concatenate([q_ref[:, lanes(g * per_group + i)] for i in range(per_group)], 0)
         for g in span]
    h_t = [h[g].T for g in span]
    k_t = [k[g].T for g in span]
    hk_t = [jnp.concatenate([h_t[g], k_t[g]], 1) for g in span]
    first = [dot(h[g], hk_t[g]) for g in span]
    gram = [first[g][:, :tok] for g in span]
    square = [jnp.where(diag, gram[g], 0.0) for g in span]
    s_col = [lax.rsqrt(jnp.sum(square[g], 1, keepdims=True) + norm_floor) for g in span]
    s_row = [lax.rsqrt(jnp.sum(square[g], 0, keepdims=True) + norm_floor) for g in span]
    beta_row = [beta_ref[g:g + 1, :] for g in span]
    beta_col = [jnp.sum(jnp.where(diag, beta_row[g], 0.0), 1, keepdims=True) for g in span]
    strict = [jnp.where(below, gram[g] * (s_col[g] * beta_col[g]) * s_row[g], 0.0) for g in span]
    key_along = [jnp.where(below, first[g][:, tok:] * s_col[g], 0.0) for g in span]
    parts = [split(strict[g]) for g in span]
    inverse = [eye - jnp.where(differ == 1, strict[g], 0.0) for g in span]
    size = 2
    stage = 0
    while size < tok:
        mask = (differ >= size) & (differ < 2 * size)
        halves = [split(inverse[g]) for g in span]
        zero = jnp.zeros((tok, tok), bf16)
        inner = [dot_three(jnp.where(mask, parts[g][0], zero), jnp.where(mask, parts[g][1], zero),
                           *halves[g]) for g in span]
        inner = [split(inner[g]) for g in span]
        inverse = [inverse[g] - dot_three(*halves[g], *inner[g]) for g in span]
        if size in (tok // 16, tok // 4):
            stage += 1
            relay_values_at(stage)
        size *= 2
    solver = [split(inverse[g] * beta_row[g]) for g in span]
    right = [split(jnp.concatenate([h[g].astype(f32) * s_col[g], key_along[g]], 1)) for g in span]
    solved = [dot_three(*solver[g], *right[g]) for g in span]
    scaled = [split(solved[g] * s_col[g]) for g in span]
    for g in span:
        base = jnp.concatenate([eye, k_t[g].astype(f32)], 1)
        turn = dot(jnp.concatenate([h_t[g], h_t[g]], 1), jnp.concatenate(scaled[g], 0))
        made = (base - turn).astype(bf16)
        maps[x, g * HD:(g + 1) * HD, :] = made[:, :HD]
        ends[g * HD:(g + 1) * HD, :] = made[:, HD:]
    row_maps(lambda copy: copy.start())

    @pl.when(more & (x == cols - 1))
    def _():
        to_next(ends, far, e_send, e_recv, z).start()
    loop(x + 1, cols,
         lambda x2: row_copy(ends, far, e_send_row, e_recv, x2, me).start())

    def own_scores(g):
        second = dot(q[g], hk_t[g])
        along = split(jnp.where(upto, second[:, :tok] * s_row[g], 0.0))
        base = jnp.concatenate([q[g].astype(f32), second[:, tok:]], 1)
        both = base - dot_three(*along, *split(solved[g]))
        turned_ref[g] = both[:, :HD].astype(bf16)
        score = jnp.where(upto, both[:, HD:] * scale, masked_score)
        top = jnp.max(score, 1, keepdims=True)
        expo = jnp.exp2(score - top)
        max_ref[g] = jnp.broadcast_to(top, max_ref.shape[1:])
        sum_ref[g] = expo
        acc_ref[g] = dot(expo.astype(bf16), v_ref[:, lanes(g)])
        prod_ref[g] = eye
        row_map[g] = eye

    def under(g):
        return slice(g * HD, (g + 1) * HD)

    def map_times(block_map, value):
        return dot(jnp.concatenate([block_map, block_map], 1), jnp.concatenate(split(value), 0))

    for g in range(0, groups, 2):
        own_scores(g)

    for dx in range(1, cols):
        wait_block(maps, m_recv, lax.rem(x + dx, cols))

    @pl.when(more & (x < cols - 1))
    def _():
        for g in span:
            def move(xr, value):
                return map_times(maps[xr, under(g), :], value)
            value = lax.fori_loop(x + 1, cols, move, ends[under(g), :].astype(f32))
            passed[z, under(g), :] = value.astype(bf16)
        to_next(passed.at[z], far, e_send, e_recv, z).start()

    for g in range(1, groups, 2):
        own_scores(g)
    for g in span:
        value = maps[0, under(g), :].astype(f32)
        for xr in range(1, cols):
            value = map_times(maps[xr, under(g), :], value)
        row_map[g] = value

    for step in range(stage + 1, rows):
        relay_values_at(step)

    def relay_keys(zr):
        block = zr * cols + x
        wait_block(far, e_recv, block)
        for dx in range(1, cols):
            relay_copy(far, e_rel, e_recv, zr, dx).start()

        @pl.when(more)
        def _():
            for g in span:
                moved = dot_two(*split(row_map[g]), far[block, under(g), :])
                passed[zr, under(g), :] = moved.astype(bf16)
            to_next(passed.at[zr], far, e_send, e_recv, zr).start()

    def absorb(block, keys_of):
        for g in span:
            score = dot(turned_ref[g], keys_of(g)) * scale
            old = max_ref[g]
            top = jnp.maximum(old, jnp.max(score, 1, keepdims=True))
            shrink = jnp.exp2(old - top)
            expo = jnp.exp2(score - top)
            max_ref[g] = top
            sum_ref[g] = sum_ref[g] * shrink + expo
            acc_ref[g] = acc_ref[g] * shrink + dot(expo.astype(bf16), vals[block, :, lanes(g)])

    def same_row(i):
        xr = x - 1 - i
        wait_block(vals, v_recv, z * cols + xr)
        wait_block(far, e_recv, z * cols + xr)

        def carried(g):
            moved = dot_two(*split(prod_ref[g]), far[z * cols + xr, under(g), :])
            return moved.astype(bf16)
        absorb(z * cols + xr, carried)
        for g in span:
            prod_ref[g] = dot_two(*split(prod_ref[g]), maps[xr, under(g), :])

    def earlier_row(i):
        zr = z - 1 - i

        def one(j):
            block = zr * cols + lax.rem(x + j, cols)

            @pl.when(j == min(1, cols - 1))
            def _():
                @pl.when(zr > 0)
                def _():
                    relay_keys(zr - 1)

            @pl.when(j > 0)
            def _():
                wait_block(vals, v_recv, block)
                wait_block(far, e_recv, block)
            absorb(block, lambda g: far[block, under(g), :])
        loop(0, cols, one)

    @pl.when(z > 0)
    def _():
        relay_keys(z - 1)
    loop(0, x, same_row)

    @pl.when((z > 0) & (x > 0))
    def _():
        for g in span:
            turned_ref[g] = map_times(turned_ref[g], prod_ref[g]).astype(bf16)
    loop(0, z, earlier_row)

    pieces = []
    for g in span:
        total = jnp.sum(sum_ref[g], 1, keepdims=True)
        mean = (acc_ref[g] / total).astype(bf16)
        pieces += [mean[i * tok:(i + 1) * tok] for i in range(per_group)]
    attended = jnp.concatenate(pieces, 1)
    width = o_ref.shape[1]
    part = width // chunks

    def part_copy(dh, c):
        at = pl.ds(c * part, part)
        return pltpu.make_async_remote_copy(
            src_ref=part_out.at[dh - 1, :, at], dst_ref=part_in.at[dh - 1, :, at],
            send_sem=p_send.at[dh - 1, c], recv_sem=p_recv.at[dh - 1, c],
            device_id={"heads": lax.rem(head + dh, peers)}, device_id_type=MESH)

    for j in range(peers):
        copy_w(j).wait()
    for dh in range(1, peers):
        there = lax.rem(head + dh, peers)
        for c in range(chunks):
            at = pl.ds(pl.multiple_of(there * width + c * part, part), part)
            part_out[dh - 1, :, c * part:(c + 1) * part] = dot(attended, w_ref[:, at]).astype(bf16)
            part_copy(dh, c).start()
    mine = []
    for c in range(chunks):
        at = pl.ds(pl.multiple_of(head * width + c * part, part), part)
        mine.append(dot(attended, w_ref[:, at]))
    for c in range(chunks):
        total = mine[c]
        for dh in range(1, peers):
            part_copy(dh, c).wait_recv()
            total = total + part_in[dh - 1, :, c * part:(c + 1) * part].astype(f32)
        o_ref[:, c * part:(c + 1) * part] = total.astype(o_ref.dtype)

    row_maps(lambda copy: copy.wait_send())
    loop(x + 1, cols,
         lambda x2: row_copy(v_ref, vals, v_send_row, v_recv, x2, me).wait_send())
    loop(x + 1, cols,
         lambda x2: row_copy(ends, far, e_send_row, e_recv, x2, me).wait_send())

    def relayed(zr):
        for dx in range(1, cols):
            relay_copy(vals, v_rel, v_recv, zr, dx).wait_send()
            relay_copy(far, e_rel, e_recv, zr, dx).wait_send()
    loop(0, z, relayed)

    def handed(zr):
        to_next(passed.at[zr], far, e_send, e_recv, zr).wait_send()
        to_next(v_ref, vals, v_send, v_recv, zr).wait_send()

    @pl.when(more)
    def _():
        loop(0, z + 1, handed)
    for dh in range(1, peers):
        for c in range(chunks):
            part_copy(dh, c).wait_send()


def per_device(n, peers, queries, keys, values, house, beta, out_weight):
    tok = queries.shape[0]
    groups = keys.shape[1] // HD
    per_group = queries.shape[1] // keys.shape[1]
    width = out_weight.shape[1] // peers
    cols = max(c for c in range(1, n + 1) if n % c == 0 and c * c <= n)
    rows = n // cols
    chunks = 2
    many = per_group * tok
    vmem = pl.BlockSpec(memory_space=pltpu.VMEM)
    hbm = pl.BlockSpec(memory_space=pltpu.HBM)
    dma = pltpu.SemaphoreType.DMA
    body = functools.partial(kernel, n, cols, peers, groups, per_group, chunks)
    inputs = (queries, keys, values, house, beta, out_weight)
    return pl.pallas_call(
        body,
        out_shape=jax.ShapeDtypeStruct((tok, width), bf16),
        in_specs=[hbm] * len(inputs),
        out_specs=vmem,
        scratch_shapes=[pltpu.VMEM(one.shape, one.dtype) for one in inputs] + [
            pltpu.VMEM((groups * HD, tok), bf16),
            pltpu.VMEM((cols, groups * HD, HD), bf16),
            pltpu.VMEM((n, groups * HD, tok), bf16),
            pltpu.VMEM((rows, groups * HD, tok), bf16),
            pltpu.VMEM((n,) + values.shape, bf16),
            pltpu.VMEM((groups, many, HD), bf16),
            pltpu.VMEM((groups, HD, HD), f32),
            pltpu.VMEM((groups, HD, HD), f32),
            pltpu.VMEM((groups, many, tok), f32),
            pltpu.VMEM((groups, many, tok), f32),
            pltpu.VMEM((groups, many, HD), f32),
            pltpu.VMEM((peers - 1, tok, width), bf16),
            pltpu.VMEM((peers - 1, tok, width), bf16),
            dma((len(inputs) - 1,)), dma((peers,)),
            dma((rows,)), dma((cols,)), dma((rows, cols)), dma((n,)),
            dma((cols,)), dma((cols,)),
            dma((rows,)), dma((cols,)), dma((rows, cols)), dma((n,)),
            dma((peers - 1, chunks)), dma((peers - 1, chunks)),
        ],
        compiler_params=pltpu.CompilerParams(
            collective_id=0, has_side_effects=True, vmem_limit_bytes=63 * 2**20
        ),
    )(*inputs)


def solution(mesh):
    in_specs = (
        P(("dp", "seq"), "heads"),
        P(("dp", "seq"), "heads"),
        P(("dp", "seq"), "heads"),
        P(("dp", "seq"), "heads"),
        P("heads", ("dp", "seq")),
        P("heads", None),
    )
    out_specs = P(("dp", "seq"), "heads")
    body = functools.partial(per_device, mesh.shape["seq"], mesh.shape["heads"])
    return jax.shard_map(
        body, mesh=mesh, in_specs=in_specs, out_specs=out_specs, check_vma=False
    )
```
